32 devices in a mesh: dp: 8 (over y, x, core), tensor: 4 (over z).
Axes of the slice: x: 2, y: 2, z: 4, core: 2. Of those that a mesh axis runs over, the one named last changes fastest.
Arguments:
- hidden_in: bfloat16 [32768, 1024], P(('dp', 'tensor')), may hold values from -6 to 6
- norm_gain: float32 [1024], replicated, may hold values from 0.5 to 1.5
- w_zx: bfloat16 [1024, 2, 2048], P(None, None, 'tensor'), may hold values from -0.1875 to 0.1875
- w_dt: bfloat16 [1024, 32], P(None, 'tensor'), may hold values from -0.1875 to 0.1875
- w_bc: bfloat16 [1024, 256], replicated, may hold values from -0.1875 to 0.1875
- conv_x: float32 [4, 2048], P(None, 'tensor'), may hold values from -3 to 3
- conv_x_bias: float32 [2048], P('tensor'), may hold values from -3 to 3
- conv_bc: float32 [4, 256], replicated, may hold values from -3 to 3
- conv_bc_bias: float32 [256], replicated, may hold values from -3 to 3
- a_log: float32 [32], P('tensor'), may hold values from 0 to 2.77
- dt_bias: float32 [32], P('tensor'), may hold values from -4.6 to -1
- d_skip: float32 [32], P('tensor'), may hold values from 0.5 to 1.5
- gate_gain: float32 [2048], P('tensor'), may hold values from 0.5 to 1.5
- w_out: bfloat16 [2048, 1024], P('tensor'), may hold values from -0.125 to 0.125
- cotangent: bfloat16 [32768, 1024], P(('dp', 'tensor')), may hold values from -6 to 6
Outputs:
- output: bfloat16 [32768, 1024], P(('dp', 'tensor'))
- input_grad: bfloat16 [32768, 1024], P(('dp', 'tensor'))
- grad_norm_gain: float32 [1024], replicated
- grad_w_zx: float32 [1024, 2, 2048], P('dp', None, 'tensor')
- grad_w_dt: float32 [1024, 32], P('dp', 'tensor')
- grad_w_bc: float32 [1024, 256], P('dp')
- grad_conv_x: float32 [4, 2048], P(None, 'tensor')
- grad_conv_x_bias: float32 [2048], P('tensor')
- grad_conv_bc: float32 [4, 256], replicated
- grad_conv_bc_bias: float32 [256], replicated
- grad_a_log: float32 [32], P('tensor')
- grad_dt_bias: float32 [32], P('tensor')
- grad_d_skip: float32 [32], P('tensor')
- grad_gate_gain: float32 [2048], P('tensor')
- grad_w_out: float32 [2048, 1024], P('tensor', 'dp')
The draws below stay inside these ranges and needn't reach their ends.
All inputs are finite; a program needn't handle non-finite values.
Results may differ from the reference program's by a relative error of at most 0.019.
Values may be sent and summed in bfloat16 or wider, within the bound.
A program may use at most 320 MiB of HBM per device.

```python
import jax
import jax.numpy as jnp
from jax import lax

D = 1024
HEADS = 32
HEAD = 64
STATE = 128
CONV = 4
BLOCK = 256
LENGTH = 1024
INNER = 2048
TOKENS = 32768


def raised(array, key, source, target, shards_of, factor):
    def block_of(dim):
        return (jnp.arange(array.shape[dim]) // (array.shape[dim] // shards_of)).reshape((-1,) + (1,) * (array.ndim - 1 - dim))

    one_side = jax.random.permutation(key, shards_of)[block_of(target)]
    second = (block_of(target) + shards_of // 2) % shards_of
    return jnp.where((block_of(source) == one_side) | (block_of(source) == second), factor * array, array)


def levels(rng, dims, cuts, low, largest):
    level, own = 1.0, jax.random.fold_in(rng, 6)
    for axis_at, parts in cuts:
        draws = jnp.exp(jax.random.uniform(jax.random.fold_in(own, axis_at), (parts,), jnp.float32, low / len(cuts), largest / len(cuts)))
        level = level * jnp.repeat(draws, dims[axis_at] // parts).reshape([-1 if axis == axis_at else 1 for axis in range(len(dims))])
    return level


def bell_draw(own_key, shape, spread, bound, shards=(), held_as=jnp.bfloat16):
    array = spread * jax.random.normal(own_key, shape, jnp.float32)
    if shards:
        array = array * levels(own_key, shape, shards, -0.22, 0.18)
    return jnp.clip(array, -bound, bound).astype(held_as)


def heavy_noise(key, shape, deviation, bound, cuts, heavy, kind=jnp.bfloat16):
    array = deviation * jax.random.normal(key, shape, jnp.float32)
    if cuts:
        array = array * levels(key, shape, cuts, -0.22, 0.18)
    return jnp.clip(raised(array, jax.random.fold_in(key, 3), *heavy), -bound, bound).astype(kind)


def setup_inputs(seed: int = 0) -> dict:
    splits = jax.random.split(jax.random.key(seed), 16)
    hidden_in = heavy_noise(splits[0], (TOKENS, D), 1.0, 6.0, ((0, 32),), (0, 1, 32, 2.75))
    norm_gain = jnp.clip(1.0 + 0.1 * jax.random.normal(splits[1], (D,), jnp.float32), 0.5, 1.5)
    w_zx = bell_draw(splits[2], (D, 2, INNER), D ** -0.5, 0.1875, ((2, 4),))
    w_dt = bell_draw(splits[3], (D, HEADS), D ** -0.5, 0.1875, ((1, 4),))
    w_bc = bell_draw(splits[4], (D, 2 * STATE), D ** -0.5, 0.1875)
    conv_x = bell_draw(splits[5], (CONV, INNER), CONV ** -0.5, 3.0, ((1, 4),), jnp.float32)
    conv_x_bias = bell_draw(splits[6], (INNER,), 0.5, 3.0, ((0, 4),), jnp.float32)
    conv_bc = bell_draw(splits[7], (CONV, 2 * STATE), CONV ** -0.5, 3.0, (), jnp.float32)
    conv_bc_bias = bell_draw(splits[8], (2 * STATE,), 0.5, 3.0, (), jnp.float32)
    a_log = jnp.clip(2.77 * jax.random.uniform(splits[9], (HEADS,), jnp.float32) ** levels(splits[9], (HEADS,), ((0, 4),), -0.2, 0.2), 0.0, 2.77)
    dt_bias = jnp.clip(-4.6 + 3.6 * jax.random.uniform(splits[10], (HEADS,), jnp.float32) ** levels(splits[10], (HEADS,), ((0, 4),), -0.2, 0.2), -4.6, -1.0)
    d_skip = jnp.clip(0.5 + 1.0 * jax.random.uniform(splits[11], (HEADS,), jnp.float32) ** levels(splits[11], (HEADS,), ((0, 4),), -0.2, 0.2), 0.5, 1.5)
    gate_gain = jnp.clip(1.0 + 0.1 * jax.random.normal(splits[12], (INNER,), jnp.float32), 0.5, 1.5)
    w_out = bell_draw(splits[13], (INNER, D), INNER ** -0.5, 0.125, ((0, 4),))
    cotangent = heavy_noise(splits[14], (TOKENS, D), 1.0, 6.0, ((0, 32),), (0, 1, 32, 2.75))
    return dict(hidden_in=hidden_in, norm_gain=norm_gain, w_zx=w_zx, w_dt=w_dt, w_bc=w_bc, conv_x=conv_x, conv_x_bias=conv_x_bias, conv_bc=conv_bc, conv_bc_bias=conv_bc_bias, a_log=a_log, dt_bias=dt_bias, d_skip=d_skip, gate_gain=gate_gain, w_out=w_out, cotangent=cotangent)


epsilon = 1e-05
highest = lax.Precision.HIGHEST

@jax.custom_vjp
def low(v):
    return lax.optimization_barrier(v.astype(jnp.bfloat16)).astype(jnp.float32)

@jax.custom_vjp
def low_back(v):
    return v

def low_keep(v):
    return (low(v), None)

def low_pass(kept, grad):
    return (grad,)

def back_keep(v):
    return (v, None)

def back_low(kept, grad):
    return (low(grad),)
low.defvjp(low_keep, low_pass)
low_back.defvjp(back_keep, back_low)

def product(left_side, right_side):
    return jnp.dot(left_side, right_side, precision=highest, preferred_element_type=jnp.float32)

def depthwise(signal, kernel, offset):
    tap_count = kernel.shape[0]
    length_now = signal.shape[1]
    padded = jnp.pad(signal, ((0, 0), (tap_count - 1, 0), (0, 0)))
    running = jnp.zeros_like(signal) + offset
    for tap_index in range(tap_count):
        running = running + kernel[tap_index] * padded[:, tap_index:tap_index + length_now, :]
    return running

def spanned_scan(heads_in, keys_in, queries_in, step_size, rates):
    seq_count = heads_in.shape[0]

    def split(values):
        shaped = values.reshape((seq_count, LENGTH // BLOCK, BLOCK) + values.shape[2:])
        return jnp.moveaxis(shaped, 1, 0)
    causal = jnp.arange(BLOCK)[:, None] >= jnp.arange(BLOCK)[None, :]

    def block_step(carried, pieces):
        input_block, key_block, query_block, step_block, rate_block = pieces
        cumulative = jnp.cumsum(rate_block, axis=1)
        gap_rates = cumulative[:, :, None, :] - cumulative[:, None, :, :]
        decays = jnp.exp(jnp.where(causal[None, :, :, None], gap_rates, -jnp.inf))
        intersection = jnp.einsum('stn,sun->stu', query_block, key_block, precision=highest)
        weights = intersection[..., None] * decays * step_block[:, None, :, :]
        inside = jnp.einsum('stuh,suhp->sthp', weights, input_block, precision=highest)
        before = jnp.einsum('stn,shpn->sthp', query_block, carried, precision=highest)
        before = before * jnp.exp(cumulative)[..., None]
        remaining = jnp.exp(cumulative[:, -1:, :] - cumulative) * step_block
        fresh = jnp.einsum('suh,suhp,sun->shpn', remaining, input_block, key_block, precision=highest)
        carried = carried * jnp.exp(cumulative[:, -1, :])[:, :, None, None] + fresh
        return (carried, inside + before)
    initial = jnp.zeros((seq_count, HEADS, HEAD, STATE), jnp.float32)
    _, by_block = lax.scan(jax.checkpoint(block_step), initial, (split(heads_in), split(keys_in), split(queries_in), split(step_size), split(rates)))
    return jnp.moveaxis(by_block, 0, 1).reshape(heads_in.shape)

def layer(hidden, norm_gain, w_zx, w_dt, w_bc, conv_x, conv_x_bias, conv_bc, conv_bc_bias, a_log, dt_bias, d_skip, gate_gain, w_out):
    seq_count = hidden.shape[0]
    inverse = lax.rsqrt(lax.optimization_barrier(jnp.mean(hidden * hidden, axis=-1, keepdims=True)) + epsilon)
    normed = low(hidden * inverse * norm_gain)
    flattened = normed.reshape(-1, D)
    gate_pre = low_back(product(flattened, w_zx[:, 0, :]))
    conv_in = low_back(product(flattened, w_zx[:, 1, :]))
    state_in = low_back(product(flattened, w_bc))
    step_raw = low_back(product(flattened, w_dt))

    def shaped(values):
        return values.reshape(seq_count, LENGTH, -1)
    mixed_in = jax.nn.silu(depthwise(shaped(conv_in), conv_x, conv_x_bias))
    state_mix = jax.nn.silu(depthwise(shaped(state_in), conv_bc, conv_bc_bias))
    step_size = jax.nn.softplus(shaped(step_raw) + dt_bias)
    rates = step_size * -jnp.exp(a_log)
    heads_in = mixed_in.reshape(seq_count, LENGTH, HEADS, HEAD)
    scanned = spanned_scan(heads_in, state_mix[..., :STATE], state_mix[..., STATE:], step_size, rates)
    scanned = scanned + d_skip[:, None] * heads_in
    gated_in = scanned.reshape(seq_count, LENGTH, INNER) * jax.nn.silu(shaped(gate_pre))
    inverse_two = lax.rsqrt(lax.optimization_barrier(jnp.mean(gated_in * gated_in, axis=-1, keepdims=True)) + epsilon)
    normed_two = low(gated_in * inverse_two * gate_gain)
    return hidden + product(normed_two.reshape(-1, INNER), w_out).reshape(hidden.shape)

def reference(hidden_in, norm_gain, w_zx, w_dt, w_bc, conv_x, conv_x_bias, conv_bc, conv_bc_bias, a_log, dt_bias, d_skip, gate_gain, w_out, cotangent):
    params = tuple((element.astype(jnp.float32) for element in (norm_gain, w_zx, w_dt, w_bc, conv_x, conv_x_bias, conv_bc, conv_bc_bias, a_log, dt_bias, d_skip, gate_gain, w_out)))
    pairs = hidden_in.reshape(-1, 2, LENGTH, D)
    cotangents = cotangent.reshape(-1, 2, LENGTH, D)

    def group(totals, inputs):
        block_in, block_cot = inputs
        result, pullback = jax.vjp(layer, block_in.astype(jnp.float32), *params)
        gradients = pullback(block_cot.astype(jnp.float32))
        totals = tuple((earlier + addend for earlier, addend in zip(totals, gradients[1:])))
        return (totals, (result.astype(jnp.bfloat16), gradients[0].astype(jnp.bfloat16)))
    zeros = tuple((jnp.zeros_like(element) for element in params))
    totals, (outputs, input_grads) = lax.scan(group, zeros, (pairs, cotangents))
    grad_norm_gain, grad_w_zx, grad_w_dt, grad_w_bc, grad_conv_x, grad_conv_x_bias, grad_conv_bc, grad_conv_bc_bias, grad_a_log, grad_dt_bias, grad_d_skip, grad_gate_gain, grad_w_out = totals
    return (outputs.reshape(-1, D), input_grads.reshape(-1, D), grad_norm_gain, grad_w_zx, grad_w_dt, grad_w_bc, grad_conv_x, grad_conv_x_bias, grad_conv_bc, grad_conv_bc_bias, grad_a_log, grad_dt_bias, grad_d_skip, grad_gate_gain, grad_w_out)
```

```python
import jax
import jax.numpy as jnp
from jax import lax
from jax.experimental import pallas as pl
from jax.experimental.pallas import tpu as pltpu
from jax.sharding import PartitionSpec as P

BLOCK = 256
LENGTH = 1024


epsilon = 1e-05
highest = lax.Precision.HIGHEST


def depthwise(signal, kernel, offset):
    tap_count = kernel.shape[0]
    length_now = signal.shape[1]
    padded = jnp.pad(signal, ((0, 0), (tap_count - 1, 0), (0, 0)))
    running = jnp.zeros_like(signal) + offset
    for tap_index in range(tap_count):
        running = running + kernel[tap_index] * padded[:, tap_index : tap_index + length_now, :]
    return running


def spanned_scan(heads_in, keys_in, queries_in, step_size, rates):
    seq_count = heads_in.shape[0]
    head_count = heads_in.shape[2]
    head_width = heads_in.shape[3]
    causal = jnp.arange(BLOCK)[:, None] >= jnp.arange(BLOCK)[None, :]
    carried = jnp.zeros((seq_count, head_count, head_width, keys_in.shape[-1]), jnp.float32)
    results = []
    for block_index in range(LENGTH // BLOCK):
        lower = block_index * BLOCK
        input_block = heads_in[:, lower : lower + BLOCK]
        key_block = keys_in[:, lower : lower + BLOCK]
        query_block = queries_in[:, lower : lower + BLOCK]
        step_block = jnp.swapaxes(step_size[:, lower : lower + BLOCK], 1, 2)
        rate_block = jnp.swapaxes(rates[:, lower : lower + BLOCK], 1, 2)
        cumulative = jnp.cumsum(rate_block, axis=2)
        gap_rates = cumulative[:, :, :, None] - cumulative[:, :, None, :]
        decays = jnp.exp(jnp.where(causal[None, None, :, :], gap_rates, -jnp.inf))
        intersection = jnp.einsum("stn,sun->stu", query_block, key_block, precision=highest)
        weights = intersection[:, None, :, :] * decays * step_block[:, :, None, :]
        inside = jnp.einsum("shtu,suhp->sthp", weights, input_block, precision=highest)
        before = jnp.einsum("stn,shpn->sthp", query_block, carried, precision=highest)
        before = before * jnp.swapaxes(jnp.exp(cumulative), 1, 2)[..., None]
        remaining = jnp.exp(cumulative[:, :, -1:] - cumulative) * step_block
        fresh = jnp.einsum(
            "shu,suhp,sun->shpn", remaining, input_block, key_block, precision=highest
        )
        carried = carried * jnp.exp(cumulative[:, :, -1])[:, :, None, None] + fresh
        results.append(inside + before)
    return jnp.concatenate(results, axis=1)


def on_device(
    hidden_in,
    norm_gain,
    w_zx,
    w_dt,
    w_bc,
    conv_x,
    conv_x_bias,
    conv_bc,
    conv_bc_bias,
    a_log,
    dt_bias,
    d_skip,
    gate_gain,
    w_out,
    cotangent,
):
    model_width = hidden_in.shape[1]
    head_count = a_log.shape[0]
    inner_local = gate_gain.shape[0]
    inner_total = inner_local * lax.axis_size("tensor")
    state_width = w_bc.shape[1] // 2
    flat_zx = w_zx.reshape(model_width, 2 * inner_local)
    residual_in = hidden_in.astype(jnp.float32)
    inverse = lax.rsqrt(jnp.mean(residual_in * residual_in, axis=-1, keepdims=True) + epsilon)
    normed = (residual_in * inverse * norm_gain).astype(jnp.bfloat16)
    gathered = lax.all_gather(normed, "tensor", axis=0, tiled=True)
    group_rows = gathered.shape[0]
    seq_count = group_rows // LENGTH
    projected = jnp.dot(gathered, flat_zx, preferred_element_type=jnp.float32)
    gate_pre = projected[:, :inner_local]
    conv_in = projected[:, inner_local:]
    state_in = jnp.dot(gathered, w_bc, preferred_element_type=jnp.float32)
    step_raw = jnp.dot(gathered, w_dt, preferred_element_type=jnp.float32)

    def shaped(values):
        return values.reshape(seq_count, LENGTH, -1)

    def local_mixer(
        conv_part,
        state_part,
        gate_part,
        step_part,
        kernel_x,
        offset_x,
        kernel_bc,
        offset_bc,
        log_rate,
        step_offset,
        skip_gain,
    ):
        mixed_in = jax.nn.silu(depthwise(shaped(conv_part), kernel_x, offset_x))
        state_mix = jax.nn.silu(depthwise(shaped(state_part), kernel_bc, offset_bc))
        step_size = jax.nn.softplus(shaped(step_part) + step_offset)
        rates = step_size * -jnp.exp(log_rate)
        heads_in = mixed_in.reshape(seq_count, LENGTH, head_count, -1)
        scanned = spanned_scan(
            heads_in, state_mix[..., :state_width], state_mix[..., state_width:], step_size, rates
        )
        scanned = scanned + skip_gain[:, None] * heads_in
        gated_in = scanned.reshape(seq_count, LENGTH, -1) * jax.nn.silu(shaped(gate_part))
        return gated_in.reshape(group_rows, -1)

    gated_in, pullback = jax.vjp(
        local_mixer,
        conv_in,
        state_in,
        gate_pre,
        step_raw,
        conv_x,
        conv_x_bias,
        conv_bc,
        conv_bc_bias,
        a_log,
        dt_bias,
        d_skip,
    )
    square_sum = lax.psum(jnp.sum(gated_in * gated_in, axis=-1), "tensor")
    inverse_two = lax.rsqrt(square_sum / inner_total + epsilon)[:, None]
    normed_two = (gated_in * inverse_two * gate_gain).astype(jnp.bfloat16)
    mixed = lax.psum_scatter(
        jnp.dot(normed_two, w_out, preferred_element_type=jnp.float32).astype(jnp.bfloat16),
        "tensor",
        scatter_dimension=0,
        tiled=True,
    ).astype(jnp.float32)
    output = (residual_in + mixed).astype(jnp.bfloat16)
    cot_rows = lax.all_gather(cotangent, "tensor", axis=0, tiled=True)
    grad_w_out = jnp.einsum("rc,rd->cd", normed_two, cot_rows, preferred_element_type=jnp.float32)
    grad_normed_two = jnp.einsum("rd,cd->rc", cot_rows, w_out, preferred_element_type=jnp.float32)
    grad_gate_gain = jnp.sum(grad_normed_two * gated_in * inverse_two, axis=0)
    scaled = grad_normed_two * gate_gain
    cross = lax.psum(jnp.sum(scaled * gated_in, axis=-1), "tensor")
    grad_gated = inverse_two * scaled - gated_in * inverse_two**3 * (cross / inner_total)[:, None]
    (
        grad_conv_in,
        grad_state_part,
        grad_gate_pre,
        grad_step_raw,
        grad_conv_x,
        grad_conv_x_bias,
        grad_conv_bc,
        grad_conv_bc_bias,
        grad_a_log,
        grad_dt_bias,
        grad_d_skip,
    ) = pullback(grad_gated)
    state_rows = lax.psum_scatter(
        grad_state_part.astype(jnp.bfloat16), "tensor", scatter_dimension=0, tiled=True
    )
    proj_low = jnp.concatenate([grad_gate_pre, grad_conv_in], axis=-1).astype(jnp.bfloat16)
    step_low = grad_step_raw.astype(jnp.bfloat16)
    step_part = step_low
    first = jnp.einsum("rk,dk->rd", proj_low, flat_zx, preferred_element_type=jnp.float32)
    grad_normed = lax.psum_scatter(
        (
            first + jnp.einsum("rh,dh->rd", step_part, w_dt, preferred_element_type=jnp.float32)
        ).astype(jnp.bfloat16),
        "tensor",
        scatter_dimension=0,
        tiled=True,
    ).astype(jnp.float32)
    grad_normed = grad_normed + jnp.einsum(
        "rk,dk->rd", state_rows, w_bc, preferred_element_type=jnp.float32
    )
    grad_norm_gain = jnp.sum(grad_normed * residual_in * inverse, axis=0)
    weighted = grad_normed * norm_gain
    grad_input = inverse * weighted - residual_in * inverse**3 * jnp.mean(
        weighted * residual_in, axis=-1, keepdims=True
    )
    input_grad = (grad_input + cotangent.astype(jnp.float32)).astype(jnp.bfloat16)
    grad_w_zx = jnp.einsum("rd,rk->dk", gathered, proj_low, preferred_element_type=jnp.float32)
    grad_w_zx = grad_w_zx.reshape(model_width, 2, inner_local)
    grad_w_dt = jnp.einsum("rd,rh->dh", gathered, step_low, preferred_element_type=jnp.float32)
    grad_w_bc = jnp.einsum("rd,rk->dk", normed, state_rows, preferred_element_type=jnp.float32)
    grad_w_zx, grad_w_dt, grad_w_out, grad_w_bc = (
        lax.psum_scatter(
            grad_w_zx.astype(jnp.bfloat16), "dp", scatter_dimension=0, tiled=True
        ).astype(jnp.float32),
        lax.psum_scatter(
            grad_w_dt.astype(jnp.bfloat16), "dp", scatter_dimension=0, tiled=True
        ).astype(jnp.float32),
        lax.psum_scatter(
            grad_w_out.astype(jnp.bfloat16), "dp", scatter_dimension=1, tiled=True
        ).astype(jnp.float32),
        lax.psum_scatter(
            grad_w_bc.astype(jnp.bfloat16), "dp", scatter_dimension=0, tiled=True
        ).astype(jnp.float32),
    )
    grad_conv_x, grad_conv_x_bias, grad_a_log, grad_dt_bias, grad_d_skip, grad_gate_gain = lax.psum(
        (grad_conv_x, grad_conv_x_bias, grad_a_log, grad_dt_bias, grad_d_skip, grad_gate_gain), "dp"
    )
    grad_norm_gain, grad_conv_bc, grad_conv_bc_bias = lax.psum(
        (grad_norm_gain, grad_conv_bc, grad_conv_bc_bias), ("dp", "tensor")
    )
    grad_w_bc = lax.psum(grad_w_bc.astype(jnp.bfloat16), "tensor").astype(jnp.float32)
    return (
        output,
        input_grad,
        grad_norm_gain,
        grad_w_zx,
        grad_w_dt,
        grad_w_bc,
        grad_conv_x,
        grad_conv_x_bias,
        grad_conv_bc,
        grad_conv_bc_bias,
        grad_a_log,
        grad_dt_bias,
        grad_d_skip,
        grad_gate_gain,
        grad_w_out,
    )


f32 = jnp.float32
bf16 = jnp.bfloat16
BLOCKS = LENGTH // BLOCK
LANES = 128


def silu_parts(values):
    gate = 1.0 / (1.0 + jnp.exp(-values))
    return values * gate, gate


def delayed(values, steps):
    if steps == 0:
        return values
    moved = pltpu.roll(values, steps, 0)
    position = lax.broadcasted_iota(jnp.int32, values.shape, 0)
    return jnp.where(position >= steps, moved, 0.0)


def advanced(values, steps):
    if steps == 0:
        return values
    length = values.shape[0]
    moved = pltpu.roll(values, length - steps, 0)
    position = lax.broadcasted_iota(jnp.int32, values.shape, 0)
    return jnp.where(position < length - steps, moved, 0.0)


def contract(left, right, left_dim, right_dim):
    return lax.dot_general(
        left, right, (((left_dim,), (right_dim,)), ((), ())), preferred_element_type=f32
    )


def causal_mask():
    later = lax.broadcasted_iota(jnp.int32, (BLOCK, BLOCK), 0)
    earlier = lax.broadcasted_iota(jnp.int32, (BLOCK, BLOCK), 1)
    return later >= earlier


def fill_products(keys, queries, products):
    for block in range(BLOCKS):
        rows = slice(block * BLOCK, (block + 1) * BLOCK)
        product = contract(queries[rows, :], keys[rows, :], 1, 1)
        products[block] = jnp.where(causal_mask(), product, 0.0)


def convolved(values, par):
    total = par[4:5, :] + par[3:4, :] * values
    for tap in range(3):
        total = total + par[tap : tap + 1, :] * delayed(values, 3 - tap)
    return total


def block_parts(block, col_ref, left):
    rows = slice(block * BLOCK, (block + 1) * BLOCK)
    col = col_ref[0, rows, :]
    cum = jnp.where(left, col[:, 0:1], col[:, 1:2])
    step = jnp.where(left, col[:, 2:3], col[:, 3:4])
    return rows, col, cum, step


def forward_kernel(z_ref, x_ref, b_ref, c_ref, par_ref, row_ref, col_ref,
                   g_ref, y_ref, st_ref, products):
    @pl.when(pl.program_id(0) == 0)
    def _():
        fill_products(b_ref, c_ref, products)

    par = par_ref[...]
    xs, _ = silu_parts(convolved(x_ref[...], par))
    left = lax.broadcasted_iota(jnp.int32, (BLOCK, LANES), 1) < LANES // 2
    state = jnp.zeros((LANES, LANES), f32)
    for block in range(BLOCKS):
        rows, col, cum, step = block_parts(block, col_ref, left)
        keys, queries = b_ref[rows, :], c_ref[rows, :]
        last = cum[BLOCK - 1 : BLOCK, :]
        stepped = xs[rows, :] * step
        stepped_low = stepped.astype(bf16)
        sides = []
        for side in range(2):
            gap = col[:, side : side + 1] - row_ref[0, side : side + 1, rows]
            weights = products[block] * jnp.exp(jnp.minimum(gap, 0.0))
            sides.append(contract(weights.astype(bf16), stepped_low, 1, 0))
        scanned = jnp.where(left, sides[0], sides[1])
        scanned = scanned + jnp.exp(cum) * contract(queries, state.astype(bf16), 1, 0)
        y_ref[rows, :] = scanned
        st_ref[0, block] = state
        gate, _ = silu_parts(z_ref[rows, :])
        g_ref[rows, :] = (scanned + par[5:6, :] * xs[rows, :]) * gate
        if block < BLOCKS - 1:
            fresh = contract(keys, (stepped * jnp.exp(last - cum)).astype(bf16), 0, 0)
            state = state * jnp.exp(last) + fresh


def backward_kernel(z_ref, x_ref, b_ref, c_ref, par_ref, row_ref, col_ref, y_ref, st_ref,
                    dyn_ref, rc_ref, dz_ref, dx_ref, pc_ref, small_ref, db_ref, dc_ref,
                    products, grad_products, dconv_ref):
    pair = pl.program_id(0)

    @pl.when(pair == 0)
    def _():
        fill_products(b_ref, c_ref, products)
        grad_products[...] = jnp.zeros_like(grad_products)
        db_ref[...] = jnp.zeros_like(db_ref)
        dc_ref[...] = jnp.zeros_like(dc_ref)

    par = par_ref[...]
    before = x_ref[...]
    conv = convolved(before, par)
    xs, conv_gate = silu_parts(conv)
    conv_slope = conv_gate * (1.0 + conv * (1.0 - conv_gate))
    left = lax.broadcasted_iota(jnp.int32, (BLOCK, LANES), 1) < LANES // 2
    row_at = lax.broadcasted_iota(jnp.int32, (BLOCK, LANES), 0)
    grad_state = jnp.zeros((LANES, LANES), f32)
    gain_sum = jnp.zeros((1, LANES), f32)
    skip_sum = jnp.zeros((1, LANES), f32)
    for block in reversed(range(BLOCKS)):
        rows, col, cum, step = block_parts(block, col_ref, left)
        keys, queries = b_ref[rows, :], c_ref[rows, :]
        last = cum[BLOCK - 1 : BLOCK, :]
        inputs = xs[rows, :]
        scanned = y_ref[rows, :]
        z = z_ref[rows, :]
        gate, gate_sig = silu_parts(z)
        full = scanned + par[5:6, :] * inputs
        gated = full * gate
        dyn = dyn_ref[rows, :]
        inverse, coef = rc_ref[rows, 0:1], rc_ref[rows, 1:2]
        scaled = dyn * inverse
        gain_sum = gain_sum + jnp.sum(scaled * gated, axis=0, keepdims=True)
        dg = scaled * par[6:7, :] - gated * coef
        dz = dg * full * (gate_sig * (1.0 + z * (1.0 - gate_sig)))
        dz_ref[rows, :] = dz.astype(bf16)
        dy = dg * gate
        skip_sum = skip_sum + jnp.sum(dy * inputs, axis=0, keepdims=True)
        stepped = inputs * step
        stepped_low = stepped.astype(bf16)
        dy_low = dy.astype(bf16)
        sides = []
        total = grad_products[block]
        for side in range(2):
            gap = col[:, side : side + 1] - row_ref[0, side : side + 1, rows]
            decay = jnp.exp(jnp.minimum(gap, 0.0))
            weights = (products[block] * decay).astype(bf16)
            sides.append(contract(weights, dy_low, 0, 0))
            own = left if side == 0 else jnp.logical_not(left)
            dy_own = jnp.where(own, dy, 0.0).astype(bf16)
            total = total + decay * contract(dy_own, stepped_low, 1, 1)
        grad_products[block] = total
        grown = jnp.exp(cum)
        decayed = jnp.exp(last - cum)
        state = st_ref[0, block]
        dy_grown = (grown * dy).astype(bf16)
        dc_ref[rows, :] += contract(dy_grown, state.astype(bf16), 1, 1)
        grad_state_low = grad_state.astype(bf16)
        late = decayed * contract(keys, grad_state_low, 1, 0)
        db_ref[rows, :] += contract((decayed * stepped).astype(bf16), grad_state_low, 1, 1)
        kept = jnp.where(left, sides[0], sides[1]) + late
        stepped_round = stepped_low.astype(f32)
        at_end = jnp.sum(stepped_round * late, axis=0, keepdims=True)
        at_end = at_end + jnp.exp(last) * jnp.sum(state * grad_state, axis=0, keepdims=True)
        dcum = dy_low.astype(f32) * scanned - stepped_round * kept
        dcum = dcum + jnp.where(row_at == BLOCK - 1, at_end, 0.0)
        dstep = inputs * kept
        sums = [
            jnp.sum(jnp.where(own, part, 0.0), axis=1, keepdims=True)
            for part in (dcum, dstep)
            for own in (left, jnp.logical_not(left))
        ]
        for place, column in enumerate(sums):
            pc_ref[0, rows, place : place + 1] = column
        dxs = par[5:6, :] * dy + step * kept
        dconv_ref[rows, :] = dxs * conv_slope[rows, :]
        if block > 0:
            grad_state = grad_state * jnp.exp(last) + contract(queries, dy_grown, 0, 0)
    dconv = dconv_ref[...]
    dx = par[3:4, :] * dconv
    small_ref[3:4, :] = jnp.sum(dconv * before, axis=0, keepdims=True)
    for tap in range(3):
        dx = dx + par[tap : tap + 1, :] * advanced(dconv, 3 - tap)
        moved = delayed(before, 3 - tap)
        small_ref[tap : tap + 1, :] = jnp.sum(dconv * moved, axis=0, keepdims=True)
    dx_ref[...] = dx.astype(bf16)
    small_ref[4:5, :] = jnp.sum(dconv, axis=0, keepdims=True)
    small_ref[5:6, :] = skip_sum
    small_ref[6:7, :] = gain_sum
    small_ref[7:8, :] = jnp.zeros_like(gain_sum)

    @pl.when(pair == pl.num_programs(0) - 1)
    def _():
        for block in range(BLOCKS):
            rows = slice(block * BLOCK, (block + 1) * BLOCK)
            grad = jnp.where(causal_mask(), grad_products[block], 0.0).astype(bf16)
            dc_ref[rows, :] += contract(grad, b_ref[rows, :], 1, 0)
            db_ref[rows, :] += contract(grad, c_ref[rows, :], 0, 0)


def lanes_of(first):
    return pl.BlockSpec((LENGTH, LANES), lambda pair: (0, first + pair))


def fixed(shape):
    return pl.BlockSpec(shape, lambda pair: (0,) * len(shape))


def per_pair(*shape):
    return pl.BlockSpec((1,) + shape, lambda pair: (pair,) + (0,) * len(shape))


def scan_specs(pairs):
    return [
        lanes_of(0),
        lanes_of(pairs),
        fixed((LENGTH, LANES)),
        fixed((LENGTH, LANES)),
        pl.BlockSpec((8, LANES), lambda pair: (0, pair)),
        per_pair(2, LENGTH),
        per_pair(LENGTH, 4),
    ]


def forward_scan(pairs, projected, keys, queries, par, rows, cols):
    width = pairs * LANES
    return pl.pallas_call(
        forward_kernel,
        grid=(pairs,),
        in_specs=scan_specs(pairs),
        out_specs=[lanes_of(0), lanes_of(0), per_pair(BLOCKS, LANES, LANES)],
        out_shape=[
            jax.ShapeDtypeStruct((LENGTH, width), f32),
            jax.ShapeDtypeStruct((LENGTH, width), f32),
            jax.ShapeDtypeStruct((pairs, BLOCKS, LANES, LANES), f32),
        ],
        scratch_shapes=[pltpu.VMEM((BLOCKS, BLOCK, BLOCK), f32)],
        compiler_params=pltpu.CompilerParams(vmem_limit_bytes=44 * 2**20),
        name="forward_scan",
    )(projected, projected, keys, queries, par, rows, cols)


def backward_scan(pairs, projected, keys, queries, par, rows, cols, scanned, states, dyn, rc):
    width = pairs * LANES
    return pl.pallas_call(
        backward_kernel,
        grid=(pairs,),
        in_specs=scan_specs(pairs)
        + [lanes_of(0), per_pair(BLOCKS, LANES, LANES), lanes_of(0), fixed((LENGTH, 2))],
        out_specs=[
            lanes_of(0),
            lanes_of(0),
            per_pair(LENGTH, 4),
            pl.BlockSpec((8, LANES), lambda pair: (0, pair)),
            fixed((LENGTH, LANES)),
            fixed((LENGTH, LANES)),
        ],
        out_shape=[
            jax.ShapeDtypeStruct((LENGTH, width), bf16),
            jax.ShapeDtypeStruct((LENGTH, width), bf16),
            jax.ShapeDtypeStruct((pairs, LENGTH, 4), f32),
            jax.ShapeDtypeStruct((8, width), f32),
            jax.ShapeDtypeStruct((LENGTH, LANES), f32),
            jax.ShapeDtypeStruct((LENGTH, LANES), f32),
        ],
        scratch_shapes=[
            pltpu.VMEM((BLOCKS, BLOCK, BLOCK), f32),
            pltpu.VMEM((BLOCKS, BLOCK, BLOCK), f32),
            pltpu.VMEM((LENGTH, LANES), f32),
        ],
        compiler_params=pltpu.CompilerParams(vmem_limit_bytes=44 * 2**20),
        name="backward_scan",
    )(projected, projected, keys, queries, par, rows, cols, scanned, states, dyn, rc)


def on_device_sequence(
    hidden_in,
    norm_gain,
    w_zx,
    w_dt,
    w_bc,
    conv_x,
    conv_x_bias,
    conv_bc,
    conv_bc_bias,
    a_log,
    dt_bias,
    d_skip,
    gate_gain,
    w_out,
    cotangent,
):
    model_width = hidden_in.shape[1]
    data_size = lax.axis_size("dp")
    group = lax.axis_size("tensor")
    data_at = lax.axis_index("dp")
    inner_local = gate_gain.shape[0]
    inner = inner_local * group
    heads_local = a_log.shape[0]
    heads = heads_local * group
    head_width = inner // heads
    pairs = inner // LANES
    share = model_width // data_size
    out_share = inner_local // data_size
    both = ("dp", "tensor")

    mine = lax.dynamic_slice_in_dim(w_zx, data_at * share, share, axis=0)
    weights_zx = lax.all_gather(mine, both, axis=0)
    weights_zx = weights_zx.reshape(data_size, group, share, 2, inner_local)
    weights_zx = weights_zx.transpose(0, 2, 3, 1, 4).reshape(model_width, 2 * inner)
    mine = lax.dynamic_slice_in_dim(w_out, data_at * out_share, out_share, axis=0)
    weights_out = lax.all_gather(mine, both, axis=0)
    weights_out = weights_out.reshape(data_size, group, out_share, model_width)
    weights_out = weights_out.transpose(1, 0, 2, 3).reshape(inner, model_width)
    packed = jnp.concatenate(
        [
            conv_x,
            conv_x_bias[None],
            gate_gain[None],
            jnp.pad(jnp.stack([a_log, dt_bias, d_skip]), ((0, 0), (0, inner_local - heads_local))),
            w_dt.astype(f32).reshape(-1, inner_local),
        ],
        axis=0,
    )
    packed = lax.all_gather(packed, "tensor", axis=0)
    wide = packed[:, :6].transpose(1, 0, 2).reshape(6, inner)
    small = packed[:, 6:9, :heads_local].transpose(1, 0, 2).reshape(3, heads)
    a_log_all, dt_bias_all, d_skip_all = small[0], small[1], small[2]
    weights_dt = packed[:, 9:].reshape(group, model_width, heads_local)
    weights_dt = weights_dt.transpose(1, 0, 2).reshape(model_width, heads).astype(bf16)

    residual_in = hidden_in.astype(f32)
    inverse = lax.rsqrt(jnp.mean(residual_in * residual_in, axis=-1, keepdims=True) + epsilon)
    normed = (residual_in * inverse * norm_gain).astype(bf16)
    state_in = jnp.dot(normed, w_bc, preferred_element_type=f32)

    def state_mixer(values, kernel, offset):
        return jax.nn.silu(depthwise(values[None], kernel, offset))[0]

    state_mix, state_pullback = jax.vjp(state_mixer, state_in, conv_bc, conv_bc_bias)
    state_low = state_mix.astype(bf16)
    keys, queries = state_low[:, :LANES], state_low[:, LANES:]
    projected = jnp.dot(normed, weights_zx, preferred_element_type=f32)
    step_raw = jnp.dot(normed, weights_dt, preferred_element_type=f32) + dt_bias_all
    step = jax.nn.softplus(step_raw)
    decay_rate = -jnp.exp(a_log_all)
    rates = (step * decay_rate).reshape(BLOCKS, BLOCK, heads)
    lower = (jnp.arange(BLOCK)[:, None] >= jnp.arange(BLOCK)[None, :]).astype(f32)
    cumulative = jnp.einsum("tu,buh->bth", lower, rates, precision=highest)
    cumulative = cumulative.reshape(LENGTH, heads)
    rows = cumulative.T.reshape(pairs, 2, LENGTH)
    cols = jnp.concatenate(
        [cumulative.reshape(LENGTH, pairs, 2), step.reshape(LENGTH, pairs, 2)], axis=-1
    ).transpose(1, 0, 2)
    par = jnp.concatenate(
        [
            wide[:5],
            jnp.repeat(d_skip_all, head_width)[None],
            wide[5:6],
            jnp.zeros((1, inner), f32),
        ],
        axis=0,
    )
    gated, scanned, states = forward_scan(pairs, projected, keys, queries, par, rows, cols)
    gain_all = wide[5]
    inverse_two = lax.rsqrt(jnp.mean(gated * gated, axis=-1, keepdims=True) + epsilon)
    normed_two = (gated * inverse_two * gain_all).astype(bf16)
    output = (
        residual_in + jnp.dot(normed_two, weights_out, preferred_element_type=f32)
    ).astype(bf16)
    grad_normed_two = jnp.einsum(
        "rd,cd->rc", cotangent, weights_out, preferred_element_type=f32
    )
    grad_w_out = jnp.einsum(
        "rc,rd->cd", normed_two, cotangent, preferred_element_type=f32
    ).astype(bf16)
    grad_w_out = grad_w_out.reshape(group, inner_local, data_size, model_width // data_size)
    grad_w_out = grad_w_out.transpose(2, 0, 1, 3).reshape(
        data_size, group * inner_local, model_width // data_size
    )
    grad_w_out = lax.psum_scatter(grad_w_out, "dp", scatter_dimension=0, tiled=True)[0]
    grad_w_out = lax.psum_scatter(grad_w_out, "tensor", scatter_dimension=0, tiled=True)
    grad_w_out = grad_w_out.astype(f32)
    cross = jnp.sum(grad_normed_two * gain_all * gated, axis=-1, keepdims=True)
    rc = jnp.concatenate([inverse_two, inverse_two**3 * cross / inner], axis=-1)
    dz, dx, pieces, grads, grad_keys, grad_queries = backward_scan(
        pairs, projected, keys, queries, par, rows, cols, scanned, states, grad_normed_two, rc
    )
    pieces = pieces.transpose(1, 0, 2)
    grad_cum = pieces[:, :, :2].reshape(BLOCKS, BLOCK, heads)
    grad_rate = jnp.einsum("tu,bth->buh", lower, grad_cum, precision=highest)
    grad_rate = grad_rate.reshape(LENGTH, heads)
    grad_step = pieces[:, :, 2:].reshape(LENGTH, heads) + grad_rate * decay_rate
    grad_a_log = jnp.sum(grad_rate * step, axis=0) * decay_rate
    grad_step = grad_step * jax.nn.sigmoid(step_raw)
    grad_dt_bias = jnp.sum(grad_step, axis=0)
    grad_d_skip = jnp.sum(grads[5].reshape(heads, head_width), axis=1)
    grad_state_in, grad_conv_bc, grad_conv_bc_bias = state_pullback(
        jnp.concatenate([grad_keys, grad_queries], axis=1)
    )
    dbc = grad_state_in.astype(bf16)
    ddt = grad_step.astype(bf16)
    proj_low = jnp.concatenate([dz, dx], axis=1)
    grad_w_zx = jnp.einsum("rd,rk->dk", normed, proj_low, preferred_element_type=f32)
    grad_w_zx = lax.psum_scatter(grad_w_zx.astype(bf16), "dp", scatter_dimension=0, tiled=True)
    grad_w_zx = grad_w_zx.reshape(share, 2, group, inner_local).transpose(2, 0, 1, 3)
    grad_w_zx = lax.psum_scatter(
        grad_w_zx.reshape(group * share, 2 * inner_local),
        "tensor",
        scatter_dimension=0,
        tiled=True,
    )
    grad_w_zx = grad_w_zx.astype(f32).reshape(share, 2, inner_local)
    side = jnp.concatenate([dbc, ddt, jnp.zeros((LENGTH, LANES - heads), bf16)], axis=1)
    grad_side = jnp.einsum("rd,rk->dk", normed, side, preferred_element_type=f32).astype(bf16)
    grad_side = lax.psum_scatter(grad_side, "dp", scatter_dimension=0, tiled=True)
    grad_side = lax.psum(grad_side, "tensor").astype(f32)
    bc_width = w_bc.shape[1]
    grad_w_bc = grad_side[:, :bc_width]
    tensor_at = lax.axis_index("tensor")
    grad_w_dt = lax.dynamic_slice_in_dim(
        grad_side, bc_width + tensor_at * heads_local, heads_local, axis=1
    )
    grad_normed = jnp.einsum("rk,dk->rd", proj_low, weights_zx, preferred_element_type=f32)
    grad_normed = grad_normed + jnp.einsum("rk,dk->rd", dbc, w_bc, preferred_element_type=f32)
    grad_normed = grad_normed + jnp.einsum(
        "rh,dh->rd", ddt, weights_dt, preferred_element_type=f32
    )
    grad_norm_gain = jnp.sum(grad_normed * residual_in * inverse, axis=0)
    weighted = grad_normed * norm_gain
    grad_input = inverse * weighted - residual_in * inverse**3 * jnp.mean(
        weighted * residual_in, axis=-1, keepdims=True
    )
    input_grad = (grad_input + cotangent.astype(f32)).astype(bf16)
    sizes = []
    flat = []
    for piece in (
        grads[:7], grad_norm_gain, grad_conv_bc, grad_conv_bc_bias,
        grad_a_log, grad_dt_bias, grad_d_skip,
    ):
        flat.append(piece.reshape(-1))
        sizes.append(flat[-1].shape[0])
    flat = jnp.concatenate(flat)
    flat = jnp.pad(flat, (0, -flat.shape[0] % 1024)).reshape(-1, LANES)
    flat = lax.psum(flat, both).reshape(-1)
    starts = [sum(sizes[:at]) for at in range(len(sizes))]
    parts = [flat[start : start + size] for start, size in zip(starts, sizes)]

    def own(values, width):
        return lax.dynamic_slice_in_dim(values, tensor_at * width, width, axis=-1)

    wide_sums = own(parts[0].reshape(7, inner), inner_local)
    return (
        output,
        input_grad,
        parts[1],
        grad_w_zx,
        grad_w_dt,
        grad_w_bc,
        wide_sums[:4],
        wide_sums[4],
        parts[2].reshape(conv_bc.shape),
        parts[3],
        own(parts[4], heads_local),
        own(parts[5], heads_local),
        own(parts[6], heads_local),
        wide_sums[6],
        grad_w_out,
    )


def solution(mesh):
    in_specs = (
        P(("dp", "tensor"), None),
        P(),
        P(None, None, "tensor"),
        P(None, "tensor"),
        P(),
        P(None, "tensor"),
        P("tensor"),
        P(),
        P(),
        P("tensor"),
        P("tensor"),
        P("tensor"),
        P("tensor"),
        P("tensor", None),
        P(("dp", "tensor"), None),
    )
    out_specs = (
        P(("dp", "tensor"), None),
        P(("dp", "tensor"), None),
        P(),
        P("dp", None, "tensor"),
        P("dp", "tensor"),
        P("dp", None),
        P(None, "tensor"),
        P("tensor"),
        P(),
        P(),
        P("tensor"),
        P("tensor"),
        P("tensor"),
        P("tensor"),
        P("tensor", "dp"),
    )

    def program(*arrays):
        whole_sequence = arrays[0].shape[0] // mesh.size == LENGTH
        return jax.shard_map(
            on_device_sequence if whole_sequence else on_device,
            mesh=mesh,
            in_specs=in_specs,
            out_specs=out_specs,
            check_vma=False,
        )(*arrays)

    return program
```
